512 devices in a mesh: grp: 64 (over z_lo, y, core), kv: 8 (over x, z_hi).
Axes of the slice: x: 4, y: 8, z: 8 (z_hi: 2, z_lo: 4; z = z_hi * 4 + z_lo), core: 2. Of those that a mesh axis runs over, the one named last changes fastest.
Arguments:
- query: bfloat16 [16384, 8192], P('grp', 'kv'), may hold values from -6 to 6
- cont_kv: bfloat16 [16384, 2048], P('grp', 'kv'), may hold values from -6 to 6
- prompt_kv: bfloat16 [64, 1024, 2048], P('grp', None, 'kv'), may hold values from -6 to 6
- out_grad: bfloat16 [16384, 8192], P('grp', 'kv'), may hold values from -6 to 6
- lengths: int32 [64], P('grp'), may hold values from 1 to 256, 10240 in all
- owners: int32 [8], P('kv'), may hold values from 0 to 63
Outputs:
- grad_query: bfloat16 [16384, 8192], P(('grp', 'kv'))
- grad_cont_kv: bfloat16 [16384, 2048], P(('grp', 'kv'))
- grad_prompt_kv: bfloat16 [64, 1024, 2048], P('grp', None, 'kv')
The draws below stay inside these ranges and needn't reach their ends.
Inputs may be any that keep to these rules, and one draw needn't show every extreme that they name: `lengths`: one continuation has exactly 256 live tokens.
All inputs are finite; a program needn't handle non-finite values. No bound on the sum of `lengths` on one device may be relied on, other than what follows from the above.
Results may differ from the reference program's by a relative error of at most 0.0077.
Values may be sent and summed in bfloat16 or wider, within the bound.
No kernel may reach another device: no remote copies, remote signals or barrier semaphores. Data moves between devices by JAX's collectives and lax.ppermute only.
A program may use at most 64 MiB of HBM per device.

```python
import math
import jax
import jax.numpy as jnp
import numpy as np
from jax import lax

HD = 128
QPK = 8
KVH = 8
HEADS = 64
P_SIZE = 1024
L = 256
CONTS = 64
N_GRP = 64


def draw_query(key, part):
    key = jax.random.fold_in(key, 11)
    base = jnp.clip(jax.random.normal(key, (CONTS * L, HEADS * HD), jnp.float32), -6.0, 6.0)
    return base.astype(jnp.bfloat16)


def draw_prompt_kv(key, part):
    key = jax.random.fold_in(key, 23)
    base = jnp.clip(jax.random.normal(key, (N_GRP, P_SIZE, KVH * 2 * HD), jnp.float32), -6.0, 6.0)
    return base.astype(jnp.bfloat16)


def place_ends(values, rng, least, largest):
    dims = values.shape
    spot = [jax.random.randint(jax.random.fold_in(rng, axis), (), 0, dims[axis]) for axis in range(len(dims))]
    values = values.at[tuple(spot)].set(least)
    longest = dims.index(max(dims))
    spot[longest] = (spot[longest] + 1) % dims[longest]
    return values.at[tuple(spot)].set(largest)


def levels(stream_key, shape, cuts, smallest, largest):
    def one(dim, parts):
        draws = jax.random.uniform(jax.random.fold_in(jax.random.fold_in(stream_key, 6), dim), (parts,), jnp.float32, smallest / len(cuts), largest / len(cuts))
        return jnp.repeat(jnp.exp(draws), shape[dim] // parts).reshape((-1,) + (1,) * (len(shape) - dim - 1))

    gain = one(*cuts[0])
    for cut in cuts[1:]:
        gain = gain * one(*cut)
    return gain


def split_up(amount, total, limit, lean):
    portions = [(1 << 20) // math.isqrt(standing ** lean) + 1 for standing in range(2, amount + 1)]
    surplus, given = total - limit - (amount - 1), [1] * (amount - 1)
    while surplus > 0:
        free = [i for i in range(amount - 1) if given[i] < limit]
        pool, budget = sum([portions[i] for i in free]), surplus
        for i in free:
            more = min(limit - given[i], max(1, budget * portions[i] // pool), surplus)
            given[i] = given[i] + more
            surplus = surplus - more
    return np.array([limit] + given)


def uneven(own_key, count, total, reach, skew):
    if count == 2:
        one = jax.random.randint(own_key, (), max(1, total - reach), min(reach, total - 1) + 1)
        return jnp.stack([one, total - one])
    sizes = jnp.asarray(split_up(count, total, reach, skew), jnp.int32)
    pairs = (count - 1) // 2
    donor, sink = sizes[1:1 + 2 * pairs:2], sizes[2:2 + 2 * pairs:2]
    room = jnp.minimum(donor - 1, reach - sink)
    shifted = jax.random.randint(jax.random.fold_in(own_key, 1), (pairs,), 0, 1 << 20) % (room + 1)
    sizes = sizes.at[1:1 + 2 * pairs:2].set(donor - shifted).at[2:2 + 2 * pairs:2].set(sink + shifted)
    return sizes[jax.random.permutation(jax.random.fold_in(own_key, 2), count)]


def normal_values(key, extent, deviation, bound, shards=(), kind=jnp.bfloat16):
    values = deviation * jax.random.normal(key, extent, jnp.float32)
    if shards:
        values = values * levels(key, extent, shards, -0.22, 0.18)
    return jnp.clip(values, -bound, bound).astype(kind)


def setup_inputs(seed: int = 0) -> dict:
    key_of = jax.random.split(jax.random.key(seed), 7)
    return {
        "query": draw_query(jax.random.fold_in(key_of[6], 71), 0),
        "cont_kv": normal_values(key_of[1], (CONTS * L, KVH * 2 * HD), 1.0, 6.0, ((0, 64), (1, 8))),
        "prompt_kv": draw_prompt_kv(jax.random.fold_in(key_of[6], 71), 0),
        "out_grad": normal_values(key_of[3], (CONTS * L, HEADS * HD), 1.0, 6.0, ((0, 64), (1, 8))),
        "lengths": uneven(key_of[4], CONTS, CONTS * L * 5 // 8, L, 1).astype(jnp.int32),
        "owners": place_ends(jax.random.randint(key_of[5], (KVH,), 0, N_GRP), jax.random.fold_in(key_of[5], 1), 0, N_GRP - 1).astype(jnp.int32),
    }


def one_continuation(q_rows, cont_rows, prompt_rows, grad_rows, length):
    scale = 1.0 / math.sqrt(HD)
    keys = jnp.concatenate([prompt_rows[:, :HD], cont_rows[:, :HD]], 0).astype(jnp.float32)
    values = jnp.concatenate([prompt_rows[:, HD:], cont_rows[:, HD:]], 0).astype(jnp.float32)
    queries = q_rows.astype(jnp.float32).reshape(L, QPK, HD)
    scores = jnp.einsum('ihd,jd->hij', queries, keys) * scale
    position = jnp.arange(L, dtype=jnp.int32)[:, None]
    key_index = jnp.arange(P_SIZE + L, dtype=jnp.int32)[None, :]
    allowed = (key_index < P_SIZE) | (key_index - P_SIZE <= position)
    scores = jnp.where(allowed[None], scores, -1e+30)
    top = lax.optimization_barrier(jnp.max(scores, axis=-1, keepdims=True))
    expo = jnp.exp(scores - top)
    probs = expo / lax.optimization_barrier(jnp.sum(expo, axis=-1, keepdims=True))
    weights = probs.astype(jnp.bfloat16).astype(jnp.float32)
    attended = jnp.einsum('hij,jd->ihd', weights, values)
    live = (jnp.arange(L, dtype=jnp.int32) < length)[:, None, None]
    live_grad = jnp.where(live, grad_rows.reshape(L, QPK, HD), jnp.zeros((), jnp.bfloat16)).astype(jnp.float32)
    delta = lax.optimization_barrier(jnp.sum(live_grad * attended, axis=-1))
    prob_grad = jnp.einsum('ihd,jd->hij', live_grad, values)
    score_grad = (probs * (prob_grad - delta.T[:, :, None]) * scale).astype(jnp.bfloat16).astype(jnp.float32)
    grad_q = jnp.einsum('hij,jd->ihd', score_grad, keys).reshape(L, QPK * HD).astype(jnp.bfloat16)
    grad_keys = jnp.einsum('hij,ihd->jd', score_grad, queries)
    grad_values = jnp.einsum('hij,ihd->jd', weights, live_grad)
    grad_both = jnp.concatenate([grad_keys, grad_values], 1)
    return (grad_q, grad_both[P_SIZE:].astype(jnp.bfloat16), grad_both[:P_SIZE])

def reference(query, cont_kv, prompt_kv, out_grad, lengths, owners):

    def per_head(head):
        owned = lax.dynamic_slice_in_dim(prompt_kv, owners[head].astype(jnp.int32), 1, 0)[0]
        prompt_rows = lax.dynamic_slice_in_dim(owned, head * 2 * HD, 2 * HD, 1)
        q_head = lax.dynamic_slice_in_dim(query, head * QPK * HD, QPK * HD, 1)
        g_head = lax.dynamic_slice_in_dim(out_grad, head * QPK * HD, QPK * HD, 1)
        c_head = lax.dynamic_slice_in_dim(cont_kv, head * 2 * HD, 2 * HD, 1)

        def step(total, index):
            start = (index * L).astype(jnp.int32)
            grad_q, grad_cont, grad_prompt = one_continuation(lax.dynamic_slice_in_dim(q_head, start, L, 0), lax.dynamic_slice_in_dim(c_head, start, L, 0), prompt_rows, lax.dynamic_slice_in_dim(g_head, start, L, 0), lengths[index])
            return (total + grad_prompt, (grad_q, grad_cont))
        total, (grad_q, grad_cont) = lax.scan(step, jnp.zeros((P_SIZE, 2 * HD), jnp.float32), jnp.arange(CONTS, dtype=jnp.int32))
        return (grad_q, grad_cont, total)
    grad_q, grad_cont, totals = lax.map(per_head, jnp.arange(KVH, dtype=jnp.int32))
    grad_query = grad_q.transpose(1, 2, 0, 3).reshape(CONTS * L, HEADS * HD)
    grad_cont_kv = grad_cont.transpose(1, 2, 0, 3).reshape(CONTS * L, KVH * 2 * HD)
    rounded = totals.astype(jnp.bfloat16).transpose(1, 0, 2)
    owned = jnp.arange(N_GRP, dtype=jnp.int32)[:, None] == owners[None, :].astype(jnp.int32)
    grad_prompt_kv = jnp.where(owned[:, None, :, None], rounded[None], jnp.zeros((), jnp.bfloat16))
    return (grad_query, grad_cont_kv, grad_prompt_kv.reshape(N_GRP, P_SIZE, KVH * 2 * HD))
```

```python
import math

import jax
import jax.numpy as jnp
from jax import lax
from jax.sharding import PartitionSpec as P

WIN = 128
CHIPS = ("zl", "y")


def spread(block, root):
    rows, width = block.shape
    peers = lax.axis_size(CHIPS)
    halves = lax.all_to_all(block.reshape(2, rows // 2, width), "core", 0, 0, tiled=True)
    half = lax.dynamic_index_in_dim(halves, root % 2, 0, keepdims=False)
    pieces = half.reshape(peers, rows // 2 // peers, width)
    pieces = lax.all_to_all(pieces, CHIPS, 0, 0, tiled=True)
    piece = lax.dynamic_index_in_dim(pieces, root // 2, 0, keepdims=True)
    return collect(piece, rows, width)


def collect(piece, rows, width):
    peers = lax.axis_size(CHIPS)
    copies = jnp.broadcast_to(piece, (peers, *piece.shape[1:]))
    half = lax.all_to_all(copies, CHIPS, 0, 0, tiled=True).reshape(rows // 2, width)
    return lax.all_gather(half, "core", tiled=True)


def total_over_group(terms):
    rows, width = terms.shape
    peers = lax.axis_size(CHIPS)
    core = lax.axis_index("core")
    halves = terms.reshape(2, rows // 2, width)
    own = lax.dynamic_index_in_dim(halves, core, 0, keepdims=False)
    other = lax.dynamic_index_in_dim(halves, 1 - core, 0, keepdims=False)
    half = own + lax.ppermute(other, "core", [(0, 1), (1, 0)])
    pieces = half.astype(jnp.bfloat16).reshape(peers, rows // 2 // peers, width)
    pieces = lax.all_to_all(pieces, CHIPS, 0, 0, tiled=True)
    piece = jnp.sum(pieces.astype(jnp.float32), axis=0, keepdims=True).astype(jnp.bfloat16)
    return collect(piece, rows, width)


def window_grads(q_rows, d_rows, keys, values, first, prompt_len, length, per_kv):
    head_dim = keys.shape[1]
    width = q_rows.shape[0] // per_kv
    scale = 1.0 / math.sqrt(head_dim)
    scores = (
        lax.dot_general(q_rows, keys, (((1,), (1,)), ((), ())), preferred_element_type=jnp.float32)
        * scale
    )
    position = first + lax.broadcasted_iota(jnp.int32, (q_rows.shape[0], 1), 0) % width
    key_index = lax.broadcasted_iota(jnp.int32, (1, keys.shape[0]), 1)
    allowed = (key_index < prompt_len) | (key_index - prompt_len <= position)
    scores = jnp.where(allowed, scores, -1e30)
    top = jnp.max(scores, axis=-1, keepdims=True)
    expo = jnp.exp(scores - top)
    probs = expo / jnp.sum(expo, axis=-1, keepdims=True)
    weights = probs.astype(jnp.bfloat16)
    attended = jnp.dot(weights, values, preferred_element_type=jnp.float32)
    live_grad = jnp.where(position < length, d_rows, jnp.zeros((), jnp.bfloat16))
    delta = jnp.sum(live_grad.astype(jnp.float32) * attended, axis=-1, keepdims=True)
    prob_grad = lax.dot_general(
        live_grad, values, (((1,), (1,)), ((), ())), preferred_element_type=jnp.float32
    )
    score_grad = (probs * (prob_grad - delta) * scale).astype(jnp.bfloat16)
    grad_q = jnp.dot(score_grad, keys, preferred_element_type=jnp.float32)
    grad_keys = lax.dot_general(
        score_grad, q_rows, (((0,), (0,)), ((), ())), preferred_element_type=jnp.float32
    )
    grad_values = lax.dot_general(
        weights, live_grad, (((0,), (0,)), ((), ())), preferred_element_type=jnp.float32
    )
    grad_q = (
        grad_q.reshape(per_kv, width, head_dim).transpose(1, 0, 2).reshape(width, per_kv * head_dim)
    )
    return (grad_q.astype(jnp.bfloat16), jnp.concatenate([grad_keys, grad_values], 1))


def head_major(block, per_kv, head_dim):
    width = block.shape[0]
    return (
        block.reshape(width, per_kv, head_dim).transpose(1, 0, 2).reshape(per_kv * width, head_dim)
    )


def body(query, cont_kv, prompt_kv, out_grad, lengths, owners):
    head_dim = cont_kv.shape[1] // 2
    seq_rows = query.shape[0]
    per_kv = query.shape[1] // head_dim
    prompt_len = prompt_kv.shape[1]
    root = owners[0]
    length = lengths[0]
    shared = spread(prompt_kv[0], root)
    keys = jnp.concatenate([shared[:, :head_dim], cont_kv[:, :head_dim]], 0)
    values = jnp.concatenate([shared[:, head_dim:], cont_kv[:, head_dim:]], 0)
    total = jnp.zeros((prompt_len + seq_rows, 2 * head_dim), jnp.float32)
    grad_blocks = []
    for window in range(seq_rows // WIN):
        first = window * WIN
        span = prompt_len + first + WIN
        q_rows = head_major(query[first : first + WIN], per_kv, head_dim)
        d_rows = head_major(out_grad[first : first + WIN], per_kv, head_dim)

        def active(q_part, d_part, key_part, value_part, first=first):
            return window_grads(
                q_part, d_part, key_part, value_part, first, prompt_len, length, per_kv
            )

        def skipped(q_part, d_part, key_part, value_part):
            return (
                jnp.zeros((q_part.shape[0] // per_kv, per_kv * head_dim), jnp.bfloat16),
                jnp.zeros((key_part.shape[0], 2 * head_dim), jnp.float32),
            )

        grad_q, grad_both = lax.cond(
            first < length, active, skipped, q_rows, d_rows, keys[:span], values[:span]
        )
        grad_blocks.append(grad_q)
        total = total.at[:span].add(grad_both)
    grad_query = jnp.concatenate(grad_blocks, 0)
    grad_cont = total[prompt_len:].astype(jnp.bfloat16)
    prompt_terms = total[:prompt_len]
    token_query, token_cont = (
        lax.all_to_all(grad_query, "kv", split_axis=0, concat_axis=1, tiled=True),
        lax.all_to_all(grad_cont, "kv", split_axis=0, concat_axis=1, tiled=True),
    )
    rounded = total_over_group(prompt_terms)
    mine = lax.axis_index(("zl", "y", "core")) == root
    grad_prompt = jnp.where(mine, rounded, jnp.zeros((), jnp.bfloat16))
    return (token_query, token_cont, grad_prompt[None])


def solution(mesh):
    groups = ("zl", "y", "core")
    fine = jax.sharding.Mesh(mesh.devices.reshape(4, 8, 2, 8), (*groups, "kv"))
    placed = (
        P(groups, "kv"),
        P(groups, "kv"),
        P(groups, None, "kv"),
        P(groups, "kv"),
        P(groups),
        P("kv"),
    )
    return jax.shard_map(
        body,
        mesh=fine,
        in_specs=placed,
        out_specs=(P((*groups, "kv"), None), P((*groups, "kv"), None), P(groups, None, "kv")),
        check_vma=False,
    )
```

```python
import math

import jax
import jax.numpy as jnp
from jax import lax
from jax.experimental import pallas as pl
from jax.experimental.pallas import tpu as pltpu
from jax.sharding import PartitionSpec as P

NT = (((1,), (1,)), ((), ()))
LOG2E = 1.4426950408889634


def dot(a, b, dims=(((1,), (0,)), ((), ()))):
    return lax.dot_general(a, b, dims, preferred_element_type=jnp.float32)


def attention_kernel(
    core_ref, length_ref, query_ref, grad_ref, prompt_ref, cont_ref,
    own_ref, other_ref, token_ref, key_ref, value_ref, turned_ref, dk_ref, dv_ref
):
    tokens, width = query_ref.shape
    prompt_len = prompt_ref.shape[0]
    hd = cont_ref.shape[1] // 2
    heads = width // hd
    peers, share, _ = token_ref.shape
    scale = 1.0 / math.sqrt(hd)
    key_ref[:prompt_len] = prompt_ref[:, :hd]
    key_ref[prompt_len:] = cont_ref[:, :hd]
    value_ref[:prompt_len] = prompt_ref[:, hd:]
    value_ref[prompt_len:] = cont_ref[:, hd:]
    turned_ref[...] = key_ref[...].astype(jnp.float32).T.astype(jnp.bfloat16)
    length = length_ref[0]
    live = lax.broadcasted_iota(jnp.int32, (tokens, hd), 0) < length
    causal = lax.broadcasted_iota(jnp.int32, (tokens, tokens), 0) <= lax.broadcasted_iota(
        jnp.int32, (tokens, tokens), 1
    )
    for head in range(heads):
        cols = slice(head * hd, (head + 1) * hd)
        q = query_ref[:, cols]
        g = jnp.where(live, grad_ref[:, cols], jnp.zeros((), jnp.bfloat16))
        s = dot(key_ref[...], q, NT)
        s = jnp.concatenate(
            [s[:prompt_len], jnp.where(causal, s[prompt_len:], -1e30)], 0
        )
        top = jnp.max(s, axis=0, keepdims=True) * (scale * LOG2E)
        e = jnp.exp2(s * (scale * LOG2E) - top)
        inv = 1.0 / jnp.sum(e, axis=0, keepdims=True)
        d = dot(value_ref[...], g, NT)
        delta = jnp.sum(e * d, axis=0, keepdims=True) * inv
        probs = e * inv
        w = probs.astype(jnp.bfloat16)
        ds = (probs * (d - delta) * scale).astype(jnp.bfloat16)
        dk = dot(ds, q)
        dv = dot(w, g)
        if head == 0:
            dk_ref[...] = dk
            dv_ref[...] = dv
        else:
            dk_ref[...] += dk
            dv_ref[...] += dv
        dq = dot(turned_ref[...], ds).T.astype(jnp.bfloat16)
        token_ref[:, :, cols] = dq.reshape(peers, share, hd)
    half = prompt_len // 2
    core = core_ref[0]
    mine = pl.ds(pl.multiple_of(core * half, half), half)
    theirs = pl.ds(pl.multiple_of((1 - core) * half, half), half)
    own_ref[:, :hd] = dk_ref[mine]
    own_ref[:, hd:] = dv_ref[mine]
    other_ref[:, :hd] = dk_ref[theirs]
    other_ref[:, hd:] = dv_ref[theirs]
    token_ref[:, :, width : width + hd] = (
        dk_ref[prompt_len:].astype(jnp.bfloat16).reshape(peers, share, hd)
    )
    token_ref[:, :, width + hd :] = (
        dv_ref[prompt_len:].astype(jnp.bfloat16).reshape(peers, share, hd)
    )


def attention_grads(query, grad, prompt, cont, core, length, peers):
    tokens, width = query.shape
    prompt_len, both = prompt.shape
    hd = both // 2
    keys = prompt_len + tokens
    return pl.pallas_call(
        attention_kernel,
        out_shape=(
            jax.ShapeDtypeStruct((prompt_len // 2, both), jnp.float32),
            jax.ShapeDtypeStruct((prompt_len // 2, both), jnp.float32),
            jax.ShapeDtypeStruct((peers, tokens // peers, width + both), jnp.bfloat16),
        ),
        in_specs=[pl.BlockSpec(memory_space=pltpu.SMEM)] * 2
        + [pl.BlockSpec(memory_space=pltpu.VMEM)] * 4,
        out_specs=[pl.BlockSpec(memory_space=pltpu.VMEM)] * 3,
        scratch_shapes=[
            pltpu.VMEM((keys, hd), jnp.bfloat16),
            pltpu.VMEM((keys, hd), jnp.bfloat16),
            pltpu.VMEM((hd, keys), jnp.bfloat16),
            pltpu.VMEM((keys, hd), jnp.float32),
            pltpu.VMEM((keys, hd), jnp.float32),
        ],
        compiler_params=pltpu.CompilerParams(vmem_limit_bytes=48 * 2**20),
    )(core, length, query, grad, prompt, cont)


CHIPS = ("zl", "y")
GROUP = ("zl", "y", "core")
SWAP = [(0, 1), (1, 0)]


def spread(block, root):
    rows, width = block.shape
    peers = lax.axis_size(CHIPS)
    halves = lax.all_to_all(block.reshape(2, rows // 2, width), "core", 0, 0, tiled=True)
    half = lax.dynamic_index_in_dim(halves, root % 2, 0, keepdims=False)
    pieces = half.reshape(peers, rows // 2 // peers, width)
    pieces = lax.all_to_all(pieces, CHIPS, 0, 0, tiled=True)
    piece = lax.dynamic_index_in_dim(pieces, root // 2, 0, keepdims=True)
    return collect(piece, rows, width)


def collect(piece, rows, width):
    peers = lax.axis_size(CHIPS)
    copies = jnp.broadcast_to(piece, (peers, *piece.shape[1:]))
    half = lax.all_to_all(copies, CHIPS, 0, 0, tiled=True).reshape(rows // 2, width)
    return lax.all_gather(half, "core", tiled=True)


def total_over_group(own, other):
    rows, width = own.shape
    peers = lax.axis_size(CHIPS)
    half = own + lax.ppermute(other, "core", SWAP)
    pieces = half.astype(jnp.bfloat16).reshape(peers, rows // peers, width)
    pieces = lax.all_to_all(pieces, CHIPS, 0, 0, tiled=True)
    piece = jnp.sum(pieces.astype(jnp.float32), axis=0, keepdims=True).astype(jnp.bfloat16)
    return collect(piece, 2 * rows, width)


def body(query, cont_kv, prompt_kv, out_grad, lengths, owners):
    root = owners[0]
    width = query.shape[1]
    core = lax.axis_index("core").astype(jnp.int32)[None]
    heads = lax.axis_size("kv")
    shared = spread(prompt_kv[0], root)
    own, other, token = attention_grads(
        query, out_grad, shared, cont_kv, core, lengths, heads
    )
    token = lax.all_to_all(token, "kv", 0, 0, tiled=True)
    token = token.transpose(1, 0, 2)
    token_query = token[:, :, :width].reshape(-1, heads * width)
    token_cont = token[:, :, width:].reshape(-1, heads * cont_kv.shape[1])
    total = total_over_group(own, other)
    mine = lax.axis_index(GROUP) == root
    grad_prompt = jnp.where(mine, total, jnp.zeros((), jnp.bfloat16))
    return (token_query, token_cont, grad_prompt[None])


def solution(mesh):
    fine = jax.sharding.Mesh(mesh.devices.reshape(4, 8, 2, 8), (*GROUP, "kv"))
    placed = (
        P(GROUP, "kv"),
        P(GROUP, "kv"),
        P(GROUP, None, "kv"),
        P(GROUP, "kv"),
        P(GROUP),
        P("kv"),
    )
    return jax.shard_map(
        body,
        mesh=fine,
        in_specs=placed,
        out_specs=(P((*GROUP, "kv"), None), P((*GROUP, "kv"), None), P(GROUP, None, "kv")),
        check_vma=False,
    )
```

```python
import math

import jax
import jax.numpy as jnp
from jax import lax
from jax.experimental import pallas as pl
from jax.experimental.pallas import tpu as pltpu
from jax.sharding import PartitionSpec as P

NT = (((1,), (1,)), ((), ()))
LOG2E = 1.4426950408889634
CHIPS = ("zl", "y")
GROUP = ("zl", "y", "core")
OWNER, LENGTH, CORE, KV, MINE = range(5)
VMEM = pl.BlockSpec(memory_space=pltpu.VMEM)
SMEM = pl.BlockSpec(memory_space=pltpu.SMEM)
ANY = pl.BlockSpec(memory_space=pl.ANY)


def like(shape, dtype=jnp.bfloat16):
    return jax.ShapeDtypeStruct(shape, dtype)


def dot(a, b, dims=(((1,), (0,)), ((), ()))):
    return lax.dot_general(a, b, dims, preferred_element_type=jnp.float32)


def attention_kernel(
    facts_ref, query_ref, grad_ref, prompt_ref, cont_ref, own_ref, other_ref, keep_ref,
    give_ref, key_ref, value_ref, turned_ref, dk_ref, dv_ref
):
    tokens, width = query_ref.shape
    prompt_len = prompt_ref.shape[0]
    hd = cont_ref.shape[1] // 2
    heads = width // hd
    ring, share, _ = keep_ref.shape
    around, side = facts_ref[KV] // 2, facts_ref[KV] % 2
    scale = 1.0 / math.sqrt(hd)
    key_ref[:prompt_len] = prompt_ref[:, :hd]
    key_ref[prompt_len:] = cont_ref[:, :hd]
    value_ref[:prompt_len] = prompt_ref[:, hd:]
    value_ref[prompt_len:] = cont_ref[:, hd:]
    turned_ref[...] = key_ref[...].astype(jnp.float32).T.astype(jnp.bfloat16)
    live = lax.broadcasted_iota(jnp.int32, (tokens, hd), 0) < facts_ref[LENGTH]
    causal = lax.broadcasted_iota(jnp.int32, (tokens, tokens), 0) <= lax.broadcasted_iota(
        jnp.int32, (tokens, tokens), 1
    )

    def hand_out(grads, columns):
        blocks = grads.reshape(ring, 2, share, hd)
        same = jnp.full((share, hd), side, jnp.int32) == 0
        for x in range(ring):
            distance = (x - around + ring) % ring
            low, high = blocks[x, 0], blocks[x, 1]
            keep_ref[distance, :, columns] = jnp.where(same, low, high)
            give_ref[distance, :, columns] = jnp.where(same, high, low)

    def products(head):
        cols = slice(head * hd, (head + 1) * hd)
        q = query_ref[:, cols]
        g = jnp.where(live, grad_ref[:, cols], jnp.zeros((), jnp.bfloat16))
        s = dot(key_ref[...], q, NT)
        s = jnp.concatenate([s[:prompt_len], jnp.where(causal, s[prompt_len:], -1e30)], 0)
        return q, g, s, dot(value_ref[...], g, NT)

    ahead = products(0)
    for head in range(heads):
        q, g, s, d = ahead
        if head + 1 < heads:
            ahead = products(head + 1)
        top = jnp.max(s, axis=0, keepdims=True) * (scale * LOG2E)
        e = jnp.exp2(s * (scale * LOG2E) - top)
        inv = 1.0 / jnp.sum(e, axis=0, keepdims=True)
        delta = jnp.sum(e * d, axis=0, keepdims=True) * inv
        probs = e * inv
        w = probs.astype(jnp.bfloat16)
        ds = (probs * (d - delta) * scale).astype(jnp.bfloat16)
        dk = dot(ds, q)
        dv = dot(w, g)
        if head == 0:
            dk_ref[...] = dk
            dv_ref[...] = dv
        else:
            dk_ref[...] += dk
            dv_ref[...] += dv
        dq = dot(turned_ref[...], ds).T.astype(jnp.bfloat16)
        hand_out(dq, slice(head * hd, (head + 1) * hd))
    half = prompt_len // 2
    mine = pl.ds(pl.multiple_of(facts_ref[CORE] * half, half), half)
    theirs = pl.ds(pl.multiple_of((1 - facts_ref[CORE]) * half, half), half)
    for ref, first in ((dk_ref, 0), (dv_ref, hd)):
        own_ref[:, first : first + hd] = ref[mine]
        other_ref[:, first : first + hd] = ref[theirs].astype(jnp.bfloat16)
        hand_out(
            ref[prompt_len:].astype(jnp.bfloat16), slice(width + first, width + first + hd)
        )


def attention_grads(query, grad, prompt, cont, facts, ring):
    tokens, width = query.shape
    prompt_len, both = prompt.shape
    hd = both // 2
    keys = prompt_len + tokens
    blocks = like((ring, tokens // ring // 2, width + both))
    return pl.pallas_call(
        attention_kernel,
        out_shape=(
            like((prompt_len // 2, both), jnp.float32),
            like((prompt_len // 2, both)),
            blocks,
            blocks,
        ),
        in_specs=[SMEM] + [VMEM] * 4,
        out_specs=[VMEM] * 4,
        scratch_shapes=[
            pltpu.VMEM((keys, hd), jnp.bfloat16),
            pltpu.VMEM((keys, hd), jnp.bfloat16),
            pltpu.VMEM((hd, keys), jnp.bfloat16),
            pltpu.VMEM((keys, hd), jnp.float32),
            pltpu.VMEM((keys, hd), jnp.float32),
        ],
        compiler_params=pltpu.CompilerParams(vmem_limit_bytes=48 * 2**20),
    )(facts, query, grad, prompt, cont)


def local_call(kernel, outs, *arrays, scratch=(), places=None):
    return pl.pallas_call(
        kernel,
        out_shape=outs,
        in_specs=places or [VMEM] * len(arrays),
        out_specs=jax.tree.map(lambda _: VMEM, outs),
        scratch_shapes=scratch,
        compiler_params=pltpu.CompilerParams(vmem_limit_bytes=8 * 2**20),
    )(*arrays)


def pick_half(facts_ref, own_ref, other_ref, half_ref, sem):
    core, half = facts_ref[CORE], half_ref.shape[0]
    rows = pl.ds(pl.multiple_of(core * half, half), half)
    here = facts_ref[OWNER] % 2 == core

    @pl.when(here)
    def _():
        copy = pltpu.make_async_copy(own_ref.at[rows], half_ref, sem)
        copy.start()
        copy.wait()

    @pl.when(jnp.logical_not(here))
    def _():
        half_ref[...] = other_ref[rows]


def pick_piece(facts_ref, pieces_ref, copies_ref):
    piece = pieces_ref[facts_ref[OWNER] // 2]
    for peer in range(copies_ref.shape[0]):
        copies_ref[peer] = piece


def add_halves(own_ref, other_ref, pieces_ref):
    half = own_ref[...] + other_ref[...].astype(jnp.float32)
    pieces_ref[...] = half.astype(jnp.bfloat16).reshape(pieces_ref.shape)


def sum_pieces(pieces_ref, keep_ref, got_ref, copies_ref, *sends):
    for distance, send in enumerate(sends):
        send[0] = keep_ref[distance + 1]
        send[1] = got_ref[distance + 1]
    piece = jnp.sum(pieces_ref[...].astype(jnp.float32), axis=0).astype(jnp.bfloat16)
    for peer in range(copies_ref.shape[0]):
        copies_ref[peer] = piece


def finish(facts_ref, total_ref, keep_ref, got_ref, *rest):
    came, (query_ref, cont_ref, prompt_ref) = rest[:-3], rest[-3:]
    ring, _, width = keep_ref.shape
    cont = cont_ref.shape[1] // (2 * ring)
    size = width - cont
    around, side = facts_ref[KV] // 2, facts_ref[KV] % 2
    for distance in range(ring):
        for slot in range(2):
            if distance:
                block = came[distance - 1].at[slot]
            else:
                block = (keep_ref, got_ref)[slot].at[0]
            head = (around - distance + ring) % ring * 2 + (side if slot == 0 else 1 - side)
            for ref, first, count in ((query_ref, 0, size), (cont_ref, size, cont)):
                columns = pl.ds(pl.multiple_of(head * count, count), count)
                ref[:, columns] = block[:, first : first + count]
    mine = facts_ref[MINE] == 1

    @pl.when(mine)
    def _():
        prompt_ref[0] = total_ref[...]

    @pl.when(jnp.logical_not(mine))
    def _():
        prompt_ref[...] = jnp.zeros_like(prompt_ref)


def collect(copies):
    half = lax.all_to_all(copies, CHIPS, 0, 0, tiled=True)
    return lax.all_gather(half.reshape(-1, half.shape[-1]), "core", tiled=True)


def swap(block, axis):
    pairs = [(i, i ^ 1) for i in range(lax.axis_size(axis))]
    return lax.ppermute(block, axis, pairs)


def body(query, cont_kv, prompt_kv, out_grad, lengths, owners):
    rows, both = prompt_kv.shape[1:]
    heads, chips = lax.axis_size("kv"), lax.axis_size(CHIPS)
    ring = heads // 2
    tokens, width = query.shape
    mine = lax.axis_index(GROUP) == owners[0]
    core, place = lax.axis_index("core"), lax.axis_index("kv")
    facts = [owners[0], lengths[0], core, place, mine]
    facts = jnp.stack([fact.astype(jnp.int32) for fact in facts])
    pieces = like((chips, rows // 2 // chips, both))

    other = swap(prompt_kv[0], "core")
    half = local_call(
        pick_half, like((rows // 2, both)), facts, prompt_kv[0], other,
        places=[SMEM, ANY, VMEM], scratch=[pltpu.SemaphoreType.DMA],
    )
    found = lax.all_to_all(half.reshape(pieces.shape), CHIPS, 0, 0, tiled=True)
    copies = local_call(pick_piece, pieces, facts, found, places=[SMEM, VMEM])
    shared = collect(copies)

    own, other, keep, give = attention_grads(query, out_grad, shared, cont_kv, facts, ring)
    other = swap(other, "core")
    got = swap(give, "kv")
    parts = local_call(add_halves, pieces, own, other)
    parts = lax.all_to_all(parts, CHIPS, 0, 0, tiled=True)
    send = like((2, *keep.shape[1:]))
    copies, *sends = local_call(sum_pieces, (pieces, *[send] * (ring - 1)), parts, keep, got)
    came = [
        lax.ppermute(block, "kv", [(i, (i + 2 * (n + 1)) % heads) for i in range(heads)])
        for n, block in enumerate(sends)
    ]
    total = collect(copies)
    outs = (
        like((tokens // heads, heads * width)),
        like((tokens // heads, heads * both)),
        like((1, rows, both)),
    )
    return local_call(
        finish, outs, facts, total, keep, got, *came, places=[SMEM] + [VMEM] * (ring + 2)
    )


def solution(mesh):
    fine = jax.sharding.Mesh(mesh.devices.reshape(4, 8, 2, 8), (*GROUP, "kv"))
    placed = (
        P(GROUP, "kv"),
        P(GROUP, "kv"),
        P(GROUP, None, "kv"),
        P(GROUP, "kv"),
        P(GROUP),
        P("kv"),
    )
    return jax.shard_map(
        body,
        mesh=fine,
        in_specs=placed,
        out_specs=(P((*GROUP, "kv"), None), P((*GROUP, "kv"), None), P(GROUP, None, "kv")),
        check_vma=False,
    )
```

```python
import math

import jax
import jax.numpy as jnp
from jax import lax
from jax.experimental import pallas as pl
from jax.experimental.pallas import tpu as pltpu
from jax.sharding import PartitionSpec as P

NT = (((1,), (1,)), ((), ()))
LOG2E = 1.4426950408889634
CHIPS = ("zl", "y")
GROUP = ("zl", "y", "core")
OWNER, LENGTH, CORE, KV, MINE = range(5)
VMEM = pl.BlockSpec(memory_space=pltpu.VMEM)
SMEM = pl.BlockSpec(memory_space=pltpu.SMEM)
ANY = pl.BlockSpec(memory_space=pl.ANY)


def like(shape, dtype=jnp.bfloat16):
    return jax.ShapeDtypeStruct(shape, dtype)


def dot(a, b, dims=(((1,), (0,)), ((), ()))):
    return lax.dot_general(a, b, dims, preferred_element_type=jnp.float32)


def attention_kernel(
    facts_ref, query_ref, grad_ref, prompt_ref, cont_ref, own_ref, other_ref, *rest
):
    tokens, width = query_ref.shape
    prompt_len = prompt_ref.shape[0]
    hd = cont_ref.shape[1] // 2
    heads = width // hd
    *token_refs, key_ref, value_ref, turned_ref, dk_ref, dv_ref, block_ref = rest
    ring, _, share, _ = block_ref.shape
    around, side = facts_ref[KV] // 2, facts_ref[KV] % 2
    scale = 1.0 / math.sqrt(hd)
    key_ref[:prompt_len] = prompt_ref[:, :hd]
    key_ref[prompt_len:] = cont_ref[:, :hd]
    value_ref[:prompt_len] = prompt_ref[:, hd:]
    value_ref[prompt_len:] = cont_ref[:, hd:]
    turned_ref[...] = key_ref[...].astype(jnp.float32).T.astype(jnp.bfloat16)
    live = lax.broadcasted_iota(jnp.int32, (tokens, hd), 0) < facts_ref[LENGTH]
    causal = lax.broadcasted_iota(jnp.int32, (tokens, tokens), 0) <= lax.broadcasted_iota(
        jnp.int32, (tokens, tokens), 1
    )

    def inputs(head):
        cols = slice(head * hd, (head + 1) * hd)
        return query_ref[:, cols], jnp.where(live, grad_ref[:, cols], jnp.zeros((), jnp.bfloat16))

    def products(head):
        q, g = inputs(head)
        s = dot(key_ref[...], q, NT)
        s = jnp.concatenate([s[:prompt_len], jnp.where(causal, s[prompt_len:], -1e30)], 0)
        return q, g, s, dot(value_ref[...], g, NT)

    def add_up(head, dk, dv):
        if head == 0:
            dk_ref[...] = dk
            dv_ref[...] = dv
        else:
            dk_ref[...] += dk
            dv_ref[...] += dv

    def store_query(head, dq):
        block_ref[..., head * hd : (head + 1) * hd] = dq.astype(jnp.bfloat16).reshape(
            ring, 2, share, hd
        )

    def shifted(head):
        q, g, s, d = products(head)
        top = jnp.max(s, axis=0, keepdims=True) * (scale * LOG2E)
        e = jnp.exp2(s * (scale * LOG2E) - top)
        inv = 1.0 / jnp.sum(e, axis=0, keepdims=True)
        delta = jnp.sum(e * d, axis=0, keepdims=True) * inv
        probs = e * inv
        w = probs.astype(jnp.bfloat16)
        ds = (probs * (d - delta) * scale).astype(jnp.bfloat16)
        add_up(head, dot(ds, q), dot(w, g))
        store_query(head, dot(turned_ref[...], ds).T)

    least, most = None, None
    ahead = products(0)
    for head in range(heads):
        q, g, s, d = ahead
        if head + 1 < heads:
            ahead = products(head + 1)
        e = jnp.exp2(s * (scale * LOG2E))
        total = jnp.sum(e, axis=0, keepdims=True)
        inv = 1.0 / total
        delta = jnp.sum(e * d, axis=0, keepdims=True) * inv
        probs = e * inv
        w = probs.astype(jnp.bfloat16)
        ds = (probs * (d - delta) * scale).astype(jnp.bfloat16)
        add_up(head, dot(ds, q), dot(w, g))
        store_query(head, dot(turned_ref[...], ds).T)
        least = total if head == 0 else jnp.minimum(least, total)
        most = total if head == 0 else jnp.maximum(most, total)
    safe = (jnp.min(least) > 2.0**-60) & (jnp.max(most) < 2.0**60)

    @pl.when(jnp.logical_not(safe))
    def _():
        for head in range(heads):
            shifted(head)

    half = prompt_len // 2
    mine = pl.ds(pl.multiple_of(facts_ref[CORE] * half, half), half)
    theirs = pl.ds(pl.multiple_of((1 - facts_ref[CORE]) * half, half), half)
    for ref, first in ((dk_ref, 0), (dv_ref, hd)):
        own_ref[:, first : first + hd] = ref[mine]
        other_ref[:, first : first + hd] = ref[theirs].astype(jnp.bfloat16)
        grads = ref[prompt_len:].astype(jnp.bfloat16)
        block_ref[..., width + first : width + first + hd] = grads.reshape(ring, 2, share, hd)
    for distance, token_ref in enumerate(token_refs):
        for slot in range(2):
            token_ref[slot] = block_ref[(around + distance) % ring, (side + slot) % 2]


def attention_grads(query, grad, prompt, cont, facts, ring):
    tokens, width = query.shape
    prompt_len, both = prompt.shape
    hd = both // 2
    keys = prompt_len + tokens
    share = tokens // ring // 2
    blocks = like((2, share, width + both))
    return pl.pallas_call(
        attention_kernel,
        out_shape=(
            like((prompt_len // 2, both), jnp.float32),
            like((prompt_len // 2, both)),
            *[blocks] * ring,
        ),
        in_specs=[SMEM] + [VMEM] * 4,
        out_specs=[VMEM] * (2 + ring),
        scratch_shapes=[
            pltpu.VMEM((keys, hd), jnp.bfloat16),
            pltpu.VMEM((keys, hd), jnp.bfloat16),
            pltpu.VMEM((hd, keys), jnp.bfloat16),
            pltpu.VMEM((keys, hd), jnp.float32),
            pltpu.VMEM((keys, hd), jnp.float32),
            pltpu.VMEM((ring, 2, share, width + both), jnp.bfloat16),
        ],
        compiler_params=pltpu.CompilerParams(vmem_limit_bytes=48 * 2**20),
    )(facts, query, grad, prompt, cont)


def local_call(kernel, outs, *arrays, scratch=(), places=None):
    return pl.pallas_call(
        kernel,
        out_shape=outs,
        in_specs=places or [VMEM] * len(arrays),
        out_specs=jax.tree.map(lambda _: VMEM, outs),
        scratch_shapes=scratch,
        compiler_params=pltpu.CompilerParams(vmem_limit_bytes=8 * 2**20),
    )(*arrays)


def pick_half(facts_ref, own_ref, other_ref, half_ref, sem):
    core, half = facts_ref[CORE], half_ref.shape[0]
    rows = pl.ds(pl.multiple_of(core * half, half), half)
    here = facts_ref[OWNER] % 2 == core

    @pl.when(here)
    def _():
        copy = pltpu.make_async_copy(own_ref.at[rows], half_ref, sem)
        copy.start()
        copy.wait()

    @pl.when(jnp.logical_not(here))
    def _():
        half_ref[...] = other_ref[rows]


def pick_piece(facts_ref, pieces_ref, copies_ref):
    piece = pieces_ref[facts_ref[OWNER] // 2]
    for peer in range(copies_ref.shape[0]):
        copies_ref[peer] = piece


def add_halves(own_ref, other_ref, pieces_ref):
    half = own_ref[...] + other_ref[...].astype(jnp.float32)
    pieces_ref[...] = half.astype(jnp.bfloat16).reshape(pieces_ref.shape)


def sum_pieces(pieces_ref, *rest):
    came, (copies_ref, give_ref) = rest[:-2], rest[-2:]
    for distance, block in enumerate(came):
        give_ref[distance] = block[1]
    piece = jnp.sum(pieces_ref[...].astype(jnp.float32), axis=0).astype(jnp.bfloat16)
    for peer in range(copies_ref.shape[0]):
        copies_ref[peer] = piece


def finish(facts_ref, total_ref, got_ref, *rest):
    came, (query_ref, cont_ref, prompt_ref) = rest[:-3], rest[-3:]
    ring, _, width = got_ref.shape
    cont = cont_ref.shape[1] // (2 * ring)
    size = width - cont
    around, side = facts_ref[KV] // 2, facts_ref[KV] % 2
    for distance in range(ring):
        source = (around - distance + ring) % ring * 2
        for block, head in (
            (came[distance].at[0], source + side),
            (got_ref.at[distance], source + 1 - side),
        ):
            for ref, first, count in ((query_ref, 0, size), (cont_ref, size, cont)):
                columns = pl.ds(pl.multiple_of(head * count, count), count)
                ref[:, columns] = block[:, first : first + count]
    mine = facts_ref[MINE] == 1

    @pl.when(mine)
    def _():
        prompt_ref[0] = total_ref[...]

    @pl.when(jnp.logical_not(mine))
    def _():
        prompt_ref[...] = jnp.zeros_like(prompt_ref)


def collect(copies):
    half = lax.all_to_all(copies, CHIPS, 0, 0, tiled=True)
    return lax.all_gather(half.reshape(-1, half.shape[-1]), "core", tiled=True)


def swap(block, axis):
    pairs = [(i, i ^ 1) for i in range(lax.axis_size(axis))]
    return lax.ppermute(block, axis, pairs)


def body(query, cont_kv, prompt_kv, out_grad, lengths, owners):
    rows, both = prompt_kv.shape[1:]
    heads, chips = lax.axis_size("kv"), lax.axis_size(CHIPS)
    ring = heads // 2
    tokens, width = query.shape
    mine = lax.axis_index(GROUP) == owners[0]
    core, place = lax.axis_index("core"), lax.axis_index("kv")
    facts = [owners[0], lengths[0], core, place, mine]
    facts = jnp.stack([fact.astype(jnp.int32) for fact in facts])
    pieces = like((chips, rows // 2 // chips, both))

    other = swap(prompt_kv[0], "core")
    half = local_call(
        pick_half, like((rows // 2, both)), facts, prompt_kv[0], other,
        places=[SMEM, ANY, VMEM], scratch=[pltpu.SemaphoreType.DMA],
    )
    found = lax.all_to_all(half.reshape(pieces.shape), CHIPS, 0, 0, tiled=True)
    copies = local_call(pick_piece, pieces, facts, found, places=[SMEM, VMEM])
    shared = collect(copies)

    own, other, *blocks = attention_grads(query, out_grad, shared, cont_kv, facts, ring)
    came = [blocks[0]] + [
        lax.ppermute(block, "kv", [(i, (i + 2 * n) % heads) for i in range(heads)])
        for n, block in enumerate(blocks)
        if n
    ]
    parts = local_call(add_halves, pieces, own, swap(other, "core"))
    parts = lax.all_to_all(parts, CHIPS, 0, 0, tiled=True)
    give = like((ring, *blocks[0].shape[1:]))
    copies, give = local_call(sum_pieces, (pieces, give), parts, *came)
    got = swap(give, "kv")
    total = collect(copies)
    outs = (
        like((tokens // heads, heads * width)),
        like((tokens // heads, heads * both)),
        like((1, rows, both)),
    )
    return local_call(
        finish, outs, facts, total, got, *came, places=[SMEM] + [VMEM] * (ring + 2)
    )


def solution(mesh):
    fine = jax.sharding.Mesh(mesh.devices.reshape(4, 8, 2, 8), (*GROUP, "kv"))
    placed = (
        P(GROUP, "kv"),
        P(GROUP, "kv"),
        P(GROUP, None, "kv"),
        P(GROUP, "kv"),
        P(GROUP),
        P("kv"),
    )
    return jax.shard_map(
        body,
        mesh=fine,
        in_specs=placed,
        out_specs=(P((*GROUP, "kv"), None), P((*GROUP, "kv"), None), P(GROUP, None, "kv")),
        check_vma=False,
    )
```

```python
import math

import jax
import jax.numpy as jnp
from jax import lax
from jax.experimental import pallas as pl
from jax.experimental.pallas import tpu as pltpu
from jax.sharding import PartitionSpec as P

NT = (((1,), (1,)), ((), ()))
LOG2E = 1.4426950408889634
CHIPS = ("zl", "y")
GROUP = ("zl", "y", "core")
OWNER, LENGTH, CORE, KV, MINE = range(5)
VMEM = pl.BlockSpec(memory_space=pltpu.VMEM)
SMEM = pl.BlockSpec(memory_space=pltpu.SMEM)
ANY = pl.BlockSpec(memory_space=pl.ANY)


def like(shape, dtype=jnp.bfloat16):
    return jax.ShapeDtypeStruct(shape, dtype)


def dot(a, b, dims=(((1,), (0,)), ((), ()))):
    return lax.dot_general(a, b, dims, preferred_element_type=jnp.float32)


def attention_kernel(
    facts_ref, query_ref, grad_ref, prompt_ref, cont_ref, own_ref, other_ref, *rest
):
    tokens, width = query_ref.shape
    prompt_len = prompt_ref.shape[0]
    hd = cont_ref.shape[1] // 2
    heads = width // hd
    *token_refs, key_ref, value_ref, turned_ref, dk_ref, dv_ref, block_ref = rest
    ring, _, share, _ = block_ref.shape
    around, side = facts_ref[KV] // 2, facts_ref[KV] % 2
    scale = 1.0 / math.sqrt(hd)
    key_ref[:prompt_len] = prompt_ref[:, :hd]
    key_ref[prompt_len:] = cont_ref[:, :hd]
    value_ref[:prompt_len] = prompt_ref[:, hd:]
    value_ref[prompt_len:] = cont_ref[:, hd:]
    turned_ref[...] = key_ref[...].astype(jnp.float32).T.astype(jnp.bfloat16)
    live = lax.broadcasted_iota(jnp.int32, (tokens, hd), 0) < facts_ref[LENGTH]
    causal = lax.broadcasted_iota(jnp.int32, (tokens, tokens), 0) <= lax.broadcasted_iota(
        jnp.int32, (tokens, tokens), 1
    )

    def inputs(head):
        cols = slice(head * hd, (head + 1) * hd)
        return query_ref[:, cols], jnp.where(live, grad_ref[:, cols], jnp.zeros((), jnp.bfloat16))

    def products(head):
        q, g = inputs(head)
        s = dot(key_ref[...], q, NT)
        s = jnp.concatenate([s[:prompt_len], jnp.where(causal, s[prompt_len:], -1e30)], 0)
        return q, g, s, dot(value_ref[...], g, NT)

    def add_up(head, dk, dv):
        if head == 0:
            dk_ref[...] = dk
            dv_ref[...] = dv
        else:
            dk_ref[...] += dk
            dv_ref[...] += dv

    def store_query(head, dq):
        block_ref[..., head * hd : (head + 1) * hd] = dq.astype(jnp.bfloat16).reshape(
            ring, 2, share, hd
        )

    def shifted(head):
        q, g, s, d = products(head)
        top = jnp.max(s, axis=0, keepdims=True) * (scale * LOG2E)
        e = jnp.exp2(s * (scale * LOG2E) - top)
        inv = 1.0 / jnp.sum(e, axis=0, keepdims=True)
        delta = jnp.sum(e * d, axis=0, keepdims=True) * inv
        probs = e * inv
        w = probs.astype(jnp.bfloat16)
        ds = (probs * (d - delta) * scale).astype(jnp.bfloat16)
        add_up(head, dot(ds, q), dot(w, g))
        store_query(head, dot(turned_ref[...], ds).T)

    least, most = None, None
    ahead = products(0)
    for head in range(heads):
        q, g, s, d = ahead
        if head + 1 < heads:
            ahead = products(head + 1)
        e = jnp.exp2(s * (scale * LOG2E))
        total = jnp.sum(e, axis=0, keepdims=True)
        inv = 1.0 / total
        delta = jnp.sum(e * d, axis=0, keepdims=True) * inv
        probs = e * inv
        w = probs.astype(jnp.bfloat16)
        ds = (probs * (d - delta) * scale).astype(jnp.bfloat16)
        add_up(head, dot(ds, q), dot(w, g))
        store_query(head, dot(turned_ref[...], ds).T)
        least = total if head == 0 else jnp.minimum(least, total)
        most = total if head == 0 else jnp.maximum(most, total)
    safe = (jnp.min(least) > 2.0**-60) & (jnp.max(most) < 2.0**60)

    @pl.when(jnp.logical_not(safe))
    def _():
        for head in range(heads):
            shifted(head)

    half = prompt_len // 2
    mine = pl.ds(pl.multiple_of(facts_ref[CORE] * half, half), half)
    theirs = pl.ds(pl.multiple_of((1 - facts_ref[CORE]) * half, half), half)
    for ref, first in ((dk_ref, 0), (dv_ref, hd)):
        own_ref[:, first : first + hd] = ref[mine]
        other_ref[:, first : first + hd] = ref[theirs].astype(jnp.bfloat16)
        grads = ref[prompt_len:].astype(jnp.bfloat16)
        block_ref[..., width + first : width + first + hd] = grads.reshape(ring, 2, share, hd)
    for slot, token_ref in enumerate(token_refs):
        for distance in range(ring):
            token_ref[distance] = block_ref[(around + distance) % ring, (side + slot) % 2]


def attention_grads(query, grad, prompt, cont, facts, ring):
    tokens, width = query.shape
    prompt_len, both = prompt.shape
    hd = both // 2
    keys = prompt_len + tokens
    share = tokens // ring // 2
    blocks = like((ring, share, width + both))
    return pl.pallas_call(
        attention_kernel,
        out_shape=(
            like((prompt_len // 2, both), jnp.float32),
            like((prompt_len // 2, both)),
            blocks,
            blocks,
        ),
        in_specs=[SMEM] + [VMEM] * 4,
        out_specs=[VMEM] * 4,
        scratch_shapes=[
            pltpu.VMEM((keys, hd), jnp.bfloat16),
            pltpu.VMEM((keys, hd), jnp.bfloat16),
            pltpu.VMEM((hd, keys), jnp.bfloat16),
            pltpu.VMEM((keys, hd), jnp.float32),
            pltpu.VMEM((keys, hd), jnp.float32),
            pltpu.VMEM((ring, 2, share, width + both), jnp.bfloat16),
        ],
        compiler_params=pltpu.CompilerParams(vmem_limit_bytes=48 * 2**20),
    )(facts, query, grad, prompt, cont)


def local_call(kernel, outs, *arrays, scratch=(), places=None):
    return pl.pallas_call(
        kernel,
        out_shape=outs,
        in_specs=places or [VMEM] * len(arrays),
        out_specs=jax.tree.map(lambda _: VMEM, outs),
        scratch_shapes=scratch,
        compiler_params=pltpu.CompilerParams(vmem_limit_bytes=8 * 2**20),
    )(*arrays)


def pick_half(facts_ref, own_ref, other_ref, half_ref, sem):
    core, half = facts_ref[CORE], half_ref.shape[0]
    rows = pl.ds(pl.multiple_of(core * half, half), half)
    here = facts_ref[OWNER] % 2 == core

    @pl.when(here)
    def _():
        copy = pltpu.make_async_copy(own_ref.at[rows], half_ref, sem)
        copy.start()
        copy.wait()

    @pl.when(jnp.logical_not(here))
    def _():
        half_ref[...] = other_ref[rows]


def pick_piece(facts_ref, pieces_ref, copies_ref):
    piece = pieces_ref[facts_ref[OWNER] // 2]
    for peer in range(copies_ref.shape[0]):
        copies_ref[peer] = piece


def add_halves(own_ref, other_ref, pieces_ref):
    half = own_ref[...] + other_ref[...].astype(jnp.float32)
    pieces_ref[...] = half.astype(jnp.bfloat16).reshape(pieces_ref.shape)


def sum_pieces(pieces_ref, keep_ref, got_ref, copies_ref, *sends):
    for distance, send in enumerate(sends):
        send[0] = keep_ref[distance + 1]
        send[1] = got_ref[distance + 1]
    piece = jnp.sum(pieces_ref[...].astype(jnp.float32), axis=0).astype(jnp.bfloat16)
    for peer in range(copies_ref.shape[0]):
        copies_ref[peer] = piece


def finish(facts_ref, total_ref, keep_ref, got_ref, *rest):
    came, (query_ref, cont_ref, prompt_ref) = rest[:-3], rest[-3:]
    ring, _, width = keep_ref.shape
    cont = cont_ref.shape[1] // (2 * ring)
    size = width - cont
    around, side = facts_ref[KV] // 2, facts_ref[KV] % 2
    for distance in range(ring):
        for slot in range(2):
            if distance:
                block = came[distance - 1].at[slot]
            else:
                block = (keep_ref, got_ref)[slot].at[0]
            head = (around - distance + ring) % ring * 2 + (side if slot == 0 else 1 - side)
            for ref, first, count in ((query_ref, 0, size), (cont_ref, size, cont)):
                columns = pl.ds(pl.multiple_of(head * count, count), count)
                ref[:, columns] = block[:, first : first + count]
    mine = facts_ref[MINE] == 1

    @pl.when(mine)
    def _():
        prompt_ref[0] = total_ref[...]

    @pl.when(jnp.logical_not(mine))
    def _():
        prompt_ref[...] = jnp.zeros_like(prompt_ref)


def collect(copies):
    half = lax.all_to_all(copies, CHIPS, 0, 0, tiled=True)
    return lax.all_gather(half.reshape(-1, half.shape[-1]), "core", tiled=True)


def swap(block, axis):
    pairs = [(i, i ^ 1) for i in range(lax.axis_size(axis))]
    return lax.ppermute(block, axis, pairs)


def body(query, cont_kv, prompt_kv, out_grad, lengths, owners):
    rows, both = prompt_kv.shape[1:]
    heads, chips = lax.axis_size("kv"), lax.axis_size(CHIPS)
    ring = heads // 2
    tokens, width = query.shape
    mine = lax.axis_index(GROUP) == owners[0]
    core, place = lax.axis_index("core"), lax.axis_index("kv")
    facts = [owners[0], lengths[0], core, place, mine]
    facts = jnp.stack([fact.astype(jnp.int32) for fact in facts])
    pieces = like((chips, rows // 2 // chips, both))

    other = swap(prompt_kv[0], "core")
    half = local_call(
        pick_half, like((rows // 2, both)), facts, prompt_kv[0], other,
        places=[SMEM, ANY, VMEM], scratch=[pltpu.SemaphoreType.DMA],
    )
    found = lax.all_to_all(half.reshape(pieces.shape), CHIPS, 0, 0, tiled=True)
    copies = local_call(pick_piece, pieces, facts, found, places=[SMEM, VMEM])
    shared = collect(copies)

    own, other, keep, give = attention_grads(query, out_grad, shared, cont_kv, facts, ring)
    got = swap(give, "kv")
    parts = local_call(add_halves, pieces, own, swap(other, "core"))
    parts = lax.fori_loop(
        0,
        jnp.minimum(lengths[0], 1),
        lambda _, block: lax.all_to_all(block, CHIPS, 0, 0, tiled=True),
        parts,
    )
    send = like((2, *keep.shape[1:]))
    copies, *sends = local_call(sum_pieces, (pieces, *[send] * (ring - 1)), parts, keep, got)
    came = [
        lax.ppermute(block, "kv", [(i, (i + 2 * (n + 1)) % heads) for i in range(heads)])
        for n, block in enumerate(sends)
    ]
    total = collect(copies)
    outs = (
        like((tokens // heads, heads * width)),
        like((tokens // heads, heads * both)),
        like((1, rows, both)),
    )
    return local_call(
        finish, outs, facts, total, keep, got, *came, places=[SMEM] + [VMEM] * (ring + 2)
    )


def solution(mesh):
    fine = jax.sharding.Mesh(mesh.devices.reshape(4, 8, 2, 8), (*GROUP, "kv"))
    placed = (
        P(GROUP, "kv"),
        P(GROUP, "kv"),
        P(GROUP, None, "kv"),
        P(GROUP, "kv"),
        P(GROUP),
        P("kv"),
    )
    return jax.shard_map(
        body,
        mesh=fine,
        in_specs=placed,
        out_specs=(P((*GROUP, "kv"), None), P((*GROUP, "kv"), None), P(GROUP, None, "kv")),
        check_vma=False,
    )
```

```python
import math

import jax
import jax.numpy as jnp
from jax import lax
from jax.experimental import pallas as pl
from jax.experimental.pallas import tpu as pltpu
from jax.sharding import PartitionSpec as P

NT = (((1,), (1,)), ((), ()))
LOG2E = 1.4426950408889634
CHIPS = ("zl", "y")
GROUP = ("zl", "y", "core")
OWNER, LENGTH, CORE, KV, MINE = range(5)
VMEM = pl.BlockSpec(memory_space=pltpu.VMEM)
SMEM = pl.BlockSpec(memory_space=pltpu.SMEM)
ANY = pl.BlockSpec(memory_space=pl.ANY)


def like(shape, dtype=jnp.bfloat16):
    return jax.ShapeDtypeStruct(shape, dtype)


def dot(a, b, dims=(((1,), (0,)), ((), ()))):
    return lax.dot_general(a, b, dims, preferred_element_type=jnp.float32)


def attention_kernel(
    facts_ref, query_ref, grad_ref, prompt_ref, cont_ref, own_ref, other_ref, *rest
):
    tokens, width = query_ref.shape
    prompt_len = prompt_ref.shape[0]
    hd = cont_ref.shape[1] // 2
    heads = width // hd
    *token_refs, key_ref, value_ref, turned_ref, dk_ref, dv_ref, block_ref = rest
    ring, _, share, _ = block_ref.shape
    around, side = facts_ref[KV] // 2, facts_ref[KV] % 2
    scale = 1.0 / math.sqrt(hd)
    key_ref[:prompt_len] = prompt_ref[:, :hd]
    key_ref[prompt_len:] = cont_ref[:, :hd]
    value_ref[:prompt_len] = prompt_ref[:, hd:]
    value_ref[prompt_len:] = cont_ref[:, hd:]
    turned_ref[...] = key_ref[...].astype(jnp.float32).T.astype(jnp.bfloat16)
    live = lax.broadcasted_iota(jnp.int32, (tokens, hd), 0) < facts_ref[LENGTH]
    causal = lax.broadcasted_iota(jnp.int32, (tokens, tokens), 0) <= lax.broadcasted_iota(
        jnp.int32, (tokens, tokens), 1
    )

    def inputs(head):
        cols = slice(head * hd, (head + 1) * hd)
        return query_ref[:, cols], jnp.where(live, grad_ref[:, cols], jnp.zeros((), jnp.bfloat16))

    def products(head):
        q, g = inputs(head)
        s = dot(key_ref[...], q, NT)
        s = jnp.concatenate([s[:prompt_len], jnp.where(causal, s[prompt_len:], -1e30)], 0)
        return q, g, s, dot(value_ref[...], g, NT)

    def add_up(head, dk, dv):
        if head == 0:
            dk_ref[...] = dk
            dv_ref[...] = dv
        else:
            dk_ref[...] += dk
            dv_ref[...] += dv

    def store_query(head, dq):
        block_ref[..., head * hd : (head + 1) * hd] = dq.astype(jnp.bfloat16).reshape(
            ring, 2, share, hd
        )

    def shifted(head):
        q, g, s, d = products(head)
        top = jnp.max(s, axis=0, keepdims=True) * (scale * LOG2E)
        e = jnp.exp2(s * (scale * LOG2E) - top)
        inv = 1.0 / jnp.sum(e, axis=0, keepdims=True)
        delta = jnp.sum(e * d, axis=0, keepdims=True) * inv
        probs = e * inv
        w = probs.astype(jnp.bfloat16)
        ds = (probs * (d - delta) * scale).astype(jnp.bfloat16)
        add_up(head, dot(ds, q), dot(w, g))
        store_query(head, dot(turned_ref[...], ds).T)

    least, most = None, None
    ahead = products(0)
    for head in range(heads):
        q, g, s, d = ahead
        if head + 1 < heads:
            ahead = products(head + 1)
        e = jnp.exp2(s * (scale * LOG2E))
        total = jnp.sum(e, axis=0, keepdims=True)
        inv = 1.0 / total
        delta = jnp.sum(e * d, axis=0, keepdims=True) * inv
        probs = e * inv
        w = probs.astype(jnp.bfloat16)
        ds = (probs * (d - delta) * scale).astype(jnp.bfloat16)
        add_up(head, dot(ds, q), dot(w, g))
        store_query(head, dot(turned_ref[...], ds).T)
        least = total if head == 0 else jnp.minimum(least, total)
        most = total if head == 0 else jnp.maximum(most, total)
    safe = (jnp.min(least) > 2.0**-60) & (jnp.max(most) < 2.0**60)

    @pl.when(jnp.logical_not(safe))
    def _():
        for head in range(heads):
            shifted(head)

    half = prompt_len // 2
    mine = pl.ds(pl.multiple_of(facts_ref[CORE] * half, half), half)
    theirs = pl.ds(pl.multiple_of((1 - facts_ref[CORE]) * half, half), half)
    for ref, first in ((dk_ref, 0), (dv_ref, hd)):
        own_ref[:, first : first + hd] = ref[mine]
        other_ref[:, first : first + hd] = ref[theirs].astype(jnp.bfloat16)
        grads = ref[prompt_len:].astype(jnp.bfloat16)
        block_ref[..., width + first : width + first + hd] = grads.reshape(ring, 2, share, hd)
    for slot, token_ref in enumerate(token_refs):
        for distance in range(ring):
            token_ref[distance] = block_ref[(around + distance) % ring, (side + slot) % 2]


def attention_grads(query, grad, prompt, cont, facts, ring):
    tokens, width = query.shape
    prompt_len, both = prompt.shape
    hd = both // 2
    keys = prompt_len + tokens
    share = tokens // ring // 2
    blocks = like((ring, share, width + both))
    return pl.pallas_call(
        attention_kernel,
        out_shape=(
            like((prompt_len // 2, both), jnp.float32),
            like((prompt_len // 2, both)),
            blocks,
            blocks,
        ),
        in_specs=[SMEM] + [VMEM] * 4,
        out_specs=[VMEM] * 4,
        scratch_shapes=[
            pltpu.VMEM((keys, hd), jnp.bfloat16),
            pltpu.VMEM((keys, hd), jnp.bfloat16),
            pltpu.VMEM((hd, keys), jnp.bfloat16),
            pltpu.VMEM((keys, hd), jnp.float32),
            pltpu.VMEM((keys, hd), jnp.float32),
            pltpu.VMEM((ring, 2, share, width + both), jnp.bfloat16),
        ],
        compiler_params=pltpu.CompilerParams(vmem_limit_bytes=48 * 2**20),
    )(facts, query, grad, prompt, cont)


def local_call(kernel, outs, *arrays, scratch=(), places=None):
    return pl.pallas_call(
        kernel,
        out_shape=outs,
        in_specs=places or [VMEM] * len(arrays),
        out_specs=jax.tree.map(lambda _: VMEM, outs),
        scratch_shapes=scratch,
        compiler_params=pltpu.CompilerParams(vmem_limit_bytes=8 * 2**20),
    )(*arrays)


def pick_half(facts_ref, own_ref, other_ref, half_ref, sem):
    core, half = facts_ref[CORE], half_ref.shape[0]
    rows = pl.ds(pl.multiple_of(core * half, half), half)
    here = facts_ref[OWNER] % 2 == core

    @pl.when(here)
    def _():
        copy = pltpu.make_async_copy(own_ref.at[rows], half_ref, sem)
        copy.start()
        copy.wait()

    @pl.when(jnp.logical_not(here))
    def _():
        half_ref[...] = other_ref[rows]


def pick_piece(facts_ref, pieces_ref, copies_ref):
    piece = pieces_ref[facts_ref[OWNER] // 2]
    for peer in range(copies_ref.shape[0]):
        copies_ref[peer] = piece


def add_halves(own_ref, other_ref, pieces_ref):
    half = own_ref[...] + other_ref[...].astype(jnp.float32)
    pieces_ref[...] = half.astype(jnp.bfloat16).reshape(pieces_ref.shape)


def sum_pieces(pieces_ref, keep_ref, got_ref, copies_ref, *sends):
    for distance, send in enumerate(sends):
        send[0] = keep_ref[distance + 1]
        send[1] = got_ref[distance + 1]
    piece = jnp.sum(pieces_ref[...].astype(jnp.float32), axis=0).astype(jnp.bfloat16)
    for peer in range(copies_ref.shape[0]):
        copies_ref[peer] = piece


def finish(facts_ref, total_ref, keep_ref, got_ref, *rest):
    came, (query_ref, cont_ref, prompt_ref) = rest[:-3], rest[-3:]
    ring, _, width = keep_ref.shape
    cont = cont_ref.shape[1] // (2 * ring)
    size = width - cont
    around, side = facts_ref[KV] // 2, facts_ref[KV] % 2
    for distance in range(ring):
        for slot in range(2):
            if distance:
                block = came[distance - 1].at[slot]
            else:
                block = (keep_ref, got_ref)[slot].at[0]
            head = (around - distance + ring) % ring * 2 + (side if slot == 0 else 1 - side)
            for ref, first, count in ((query_ref, 0, size), (cont_ref, size, cont)):
                columns = pl.ds(pl.multiple_of(head * count, count), count)
                ref[:, columns] = block[:, first : first + count]
    mine = facts_ref[MINE] == 1

    @pl.when(mine)
    def _():
        prompt_ref[0] = total_ref[...]

    @pl.when(jnp.logical_not(mine))
    def _():
        prompt_ref[...] = jnp.zeros_like(prompt_ref)


def collect(copies):
    half = lax.all_to_all(copies, CHIPS, 0, 0, tiled=True)
    return lax.all_gather(half.reshape(-1, half.shape[-1]), "core", tiled=True)


def swap(block, axis):
    pairs = [(i, i ^ 1) for i in range(lax.axis_size(axis))]
    return lax.ppermute(block, axis, pairs)


def body(query, cont_kv, prompt_kv, out_grad, lengths, owners):
    rows, both = prompt_kv.shape[1:]
    heads, chips = lax.axis_size("kv"), lax.axis_size(CHIPS)
    ring = heads // 2
    tokens, width = query.shape
    mine = lax.axis_index(GROUP) == owners[0]
    core, place = lax.axis_index("core"), lax.axis_index("kv")
    facts = [owners[0], lengths[0], core, place, mine]
    facts = jnp.stack([fact.astype(jnp.int32) for fact in facts])
    pieces = like((chips, rows // 2 // chips, both))

    other = swap(prompt_kv[0], "core")
    half = local_call(
        pick_half, like((rows // 2, both)), facts, prompt_kv[0], other,
        places=[SMEM, ANY, VMEM], scratch=[pltpu.SemaphoreType.DMA],
    )
    found = lax.all_to_all(half.reshape(pieces.shape), CHIPS, 0, 0, tiled=True)
    copies = local_call(pick_piece, pieces, facts, found, places=[SMEM, VMEM])
    shared = collect(copies)

    own, other, keep, give = attention_grads(query, out_grad, shared, cont_kv, facts, ring)
    other = swap(other, "core")
    got = swap(give, "kv")
    parts = local_call(add_halves, pieces, own, other)
    parts = lax.cond(
        lengths[0] > 0,
        lambda block: lax.all_to_all(block, CHIPS, 0, 0, tiled=True),
        lambda block: block,
        parts,
    )
    send = like((2, *keep.shape[1:]))
    copies, *sends = local_call(sum_pieces, (pieces, *[send] * (ring - 1)), parts, keep, got)
    came = [
        lax.ppermute(block, "kv", [(i, (i + 2 * (n + 1)) % heads) for i in range(heads)])
        for n, block in enumerate(sends)
    ]
    total = collect(copies)
    outs = (
        like((tokens // heads, heads * width)),
        like((tokens // heads, heads * both)),
        like((1, rows, both)),
    )
    return local_call(
        finish, outs, facts, total, keep, got, *came, places=[SMEM] + [VMEM] * (ring + 2)
    )


def solution(mesh):
    fine = jax.sharding.Mesh(mesh.devices.reshape(4, 8, 2, 8), (*GROUP, "kv"))
    placed = (
        P(GROUP, "kv"),
        P(GROUP, "kv"),
        P(GROUP, None, "kv"),
        P(GROUP, "kv"),
        P(GROUP),
        P("kv"),
    )
    return jax.shard_map(
        body,
        mesh=fine,
        in_specs=placed,
        out_specs=(P((*GROUP, "kv"), None), P((*GROUP, "kv"), None), P(GROUP, None, "kv")),
        check_vma=False,
    )
```

```python
import math

import jax
import jax.numpy as jnp
from jax import lax
from jax.experimental import pallas as pl
from jax.experimental.pallas import tpu as pltpu
from jax.sharding import PartitionSpec as P

NT = (((1,), (1,)), ((), ()))
LOG2E = 1.4426950408889634
CHIPS = ("zl", "y")
GROUP = ("zl", "y", "core")
OWNER, LENGTH, CORE, KV, MINE = range(5)
VMEM = pl.BlockSpec(memory_space=pltpu.VMEM)
SMEM = pl.BlockSpec(memory_space=pltpu.SMEM)
ANY = pl.BlockSpec(memory_space=pl.ANY)


def like(shape, dtype=jnp.bfloat16):
    return jax.ShapeDtypeStruct(shape, dtype)


def dot(a, b, dims=(((1,), (0,)), ((), ()))):
    return lax.dot_general(a, b, dims, preferred_element_type=jnp.float32)


def attention_kernel(
    facts_ref, query_ref, grad_ref, prompt_ref, cont_ref, own_ref, other_ref, *rest
):
    tokens, width = query_ref.shape
    prompt_len = prompt_ref.shape[0]
    hd = cont_ref.shape[1] // 2
    heads = width // hd
    *token_refs, key_ref, value_ref, turned_ref, dk_ref, dv_ref, block_ref = rest
    ring, _, share, _ = block_ref.shape
    around, side = facts_ref[KV] // 2, facts_ref[KV] % 2
    scale = 1.0 / math.sqrt(hd)
    key_ref[:prompt_len] = prompt_ref[:, :hd]
    key_ref[prompt_len:] = cont_ref[:, :hd]
    value_ref[:prompt_len] = prompt_ref[:, hd:]
    value_ref[prompt_len:] = cont_ref[:, hd:]
    turned_ref[...] = key_ref[...].astype(jnp.float32).T.astype(jnp.bfloat16)
    live = lax.broadcasted_iota(jnp.int32, (tokens, hd), 0) < facts_ref[LENGTH]
    causal = lax.broadcasted_iota(jnp.int32, (tokens, tokens), 0) <= lax.broadcasted_iota(
        jnp.int32, (tokens, tokens), 1
    )

    def inputs(head):
        cols = slice(head * hd, (head + 1) * hd)
        return query_ref[:, cols], jnp.where(live, grad_ref[:, cols], jnp.zeros((), jnp.bfloat16))

    def products(head):
        q, g = inputs(head)
        s = dot(key_ref[...], q, NT)
        s = jnp.concatenate([s[:prompt_len], jnp.where(causal, s[prompt_len:], -1e30)], 0)
        return q, g, s, dot(value_ref[...], g, NT)

    def add_up(head, dk, dv):
        if head == 0:
            dk_ref[...] = dk
            dv_ref[...] = dv
        else:
            dk_ref[...] += dk
            dv_ref[...] += dv

    def store_query(head, dq):
        block_ref[..., head * hd : (head + 1) * hd] = dq.astype(jnp.bfloat16).reshape(
            ring, 2, share, hd
        )

    def shifted(head):
        q, g, s, d = products(head)
        top = jnp.max(s, axis=0, keepdims=True) * (scale * LOG2E)
        e = jnp.exp2(s * (scale * LOG2E) - top)
        inv = 1.0 / jnp.sum(e, axis=0, keepdims=True)
        delta = jnp.sum(e * d, axis=0, keepdims=True) * inv
        probs = e * inv
        w = probs.astype(jnp.bfloat16)
        ds = (probs * (d - delta) * scale).astype(jnp.bfloat16)
        add_up(head, dot(ds, q), dot(w, g))
        store_query(head, dot(turned_ref[...], ds).T)

    least, most = None, None
    ahead = products(0)
    for head in range(heads):
        q, g, s, d = ahead
        if head + 1 < heads:
            ahead = products(head + 1)
        e = jnp.exp2(s * (scale * LOG2E))
        total = jnp.sum(e, axis=0, keepdims=True)
        inv = 1.0 / total
        delta = jnp.sum(e * d, axis=0, keepdims=True) * inv
        probs = e * inv
        w = probs.astype(jnp.bfloat16)
        ds = (probs * (d - delta) * scale).astype(jnp.bfloat16)
        add_up(head, dot(ds, q), dot(w, g))
        store_query(head, dot(turned_ref[...], ds).T)
        least = total if head == 0 else jnp.minimum(least, total)
        most = total if head == 0 else jnp.maximum(most, total)
    safe = (jnp.min(least) > 2.0**-60) & (jnp.max(most) < 2.0**60)

    @pl.when(jnp.logical_not(safe))
    def _():
        for head in range(heads):
            shifted(head)

    half = prompt_len // 2
    mine = pl.ds(pl.multiple_of(facts_ref[CORE] * half, half), half)
    theirs = pl.ds(pl.multiple_of((1 - facts_ref[CORE]) * half, half), half)
    for ref, first in ((dk_ref, 0), (dv_ref, hd)):
        own_ref[:, first : first + hd] = ref[mine]
        other_ref[:, first : first + hd] = ref[theirs].astype(jnp.bfloat16)
        grads = ref[prompt_len:].astype(jnp.bfloat16)
        block_ref[..., width + first : width + first + hd] = grads.reshape(ring, 2, share, hd)
    for slot, token_ref in enumerate(token_refs):
        for distance in range(ring):
            token_ref[distance] = block_ref[(around + distance) % ring, (side + slot) % 2]


def attention_grads(query, grad, prompt, cont, facts, ring):
    tokens, width = query.shape
    prompt_len, both = prompt.shape
    hd = both // 2
    keys = prompt_len + tokens
    share = tokens // ring // 2
    blocks = like((ring, share, width + both))
    return pl.pallas_call(
        attention_kernel,
        out_shape=(
            like((prompt_len // 2, both), jnp.float32),
            like((prompt_len // 2, both)),
            blocks,
            blocks,
        ),
        in_specs=[SMEM] + [VMEM] * 4,
        out_specs=[VMEM] * 4,
        scratch_shapes=[
            pltpu.VMEM((keys, hd), jnp.bfloat16),
            pltpu.VMEM((keys, hd), jnp.bfloat16),
            pltpu.VMEM((hd, keys), jnp.bfloat16),
            pltpu.VMEM((keys, hd), jnp.float32),
            pltpu.VMEM((keys, hd), jnp.float32),
            pltpu.VMEM((ring, 2, share, width + both), jnp.bfloat16),
        ],
        compiler_params=pltpu.CompilerParams(vmem_limit_bytes=48 * 2**20),
    )(facts, query, grad, prompt, cont)


def local_call(kernel, outs, *arrays, scratch=(), places=None):
    return pl.pallas_call(
        kernel,
        out_shape=outs,
        in_specs=places or [VMEM] * len(arrays),
        out_specs=jax.tree.map(lambda _: VMEM, outs),
        scratch_shapes=scratch,
        compiler_params=pltpu.CompilerParams(vmem_limit_bytes=8 * 2**20),
    )(*arrays)


def pick_half(facts_ref, own_ref, other_ref, half_ref, sem):
    core, half = facts_ref[CORE], half_ref.shape[0]
    rows = pl.ds(pl.multiple_of(core * half, half), half)
    here = facts_ref[OWNER] % 2 == core

    @pl.when(here)
    def _():
        copy = pltpu.make_async_copy(own_ref.at[rows], half_ref, sem)
        copy.start()
        copy.wait()

    @pl.when(jnp.logical_not(here))
    def _():
        half_ref[...] = other_ref[rows]


def pick_piece(facts_ref, pieces_ref, copies_ref):
    piece = pieces_ref[facts_ref[OWNER] // 2]
    for peer in range(copies_ref.shape[0]):
        copies_ref[peer] = piece


def add_halves(facts_ref, own_ref, others_ref, pieces_ref):
    half = own_ref[...] + others_ref[1 - facts_ref[CORE]].astype(jnp.float32)
    pieces_ref[...] = half.astype(jnp.bfloat16).reshape(pieces_ref.shape)


def sum_pieces(pieces_ref, keep_ref, got_ref, copies_ref, *sends):
    for distance, send in enumerate(sends):
        send[0] = keep_ref[distance + 1]
        send[1] = got_ref[distance + 1]
    piece = jnp.sum(pieces_ref[...].astype(jnp.float32), axis=0).astype(jnp.bfloat16)
    for peer in range(copies_ref.shape[0]):
        copies_ref[peer] = piece


def finish(facts_ref, total_ref, keep_ref, got_ref, *rest):
    came, (query_ref, cont_ref, prompt_ref) = rest[:-3], rest[-3:]
    ring, _, width = keep_ref.shape
    cont = cont_ref.shape[1] // (2 * ring)
    size = width - cont
    around, side = facts_ref[KV] // 2, facts_ref[KV] % 2
    for distance in range(ring):
        for slot in range(2):
            if distance:
                block = came[distance - 1].at[slot]
            else:
                block = (keep_ref, got_ref)[slot].at[0]
            head = (around - distance + ring) % ring * 2 + (side if slot == 0 else 1 - side)
            for ref, first, count in ((query_ref, 0, size), (cont_ref, size, cont)):
                columns = pl.ds(pl.multiple_of(head * count, count), count)
                ref[:, columns] = block[:, first : first + count]
    mine = facts_ref[MINE] == 1

    @pl.when(mine)
    def _():
        prompt_ref[0] = total_ref[...]

    @pl.when(jnp.logical_not(mine))
    def _():
        prompt_ref[...] = jnp.zeros_like(prompt_ref)


def collect(copies):
    half = lax.all_to_all(copies, CHIPS, 0, 0, tiled=True)
    return lax.all_gather(half.reshape(-1, half.shape[-1]), "core", tiled=True)


def swap(block, axis):
    pairs = [(i, i ^ 1) for i in range(lax.axis_size(axis))]
    return lax.ppermute(block, axis, pairs)


def body(query, cont_kv, prompt_kv, out_grad, lengths, owners):
    rows, both = prompt_kv.shape[1:]
    heads, chips = lax.axis_size("kv"), lax.axis_size(CHIPS)
    ring = heads // 2
    tokens, width = query.shape
    mine = lax.axis_index(GROUP) == owners[0]
    core, place = lax.axis_index("core"), lax.axis_index("kv")
    facts = [owners[0], lengths[0], core, place, mine]
    facts = jnp.stack([fact.astype(jnp.int32) for fact in facts])
    pieces = like((chips, rows // 2 // chips, both))

    other = swap(prompt_kv[0], "core")
    half = local_call(
        pick_half, like((rows // 2, both)), facts, prompt_kv[0], other,
        places=[SMEM, ANY, VMEM], scratch=[pltpu.SemaphoreType.DMA],
    )
    found = lax.all_to_all(half.reshape(pieces.shape), CHIPS, 0, 0, tiled=True)
    copies = local_call(pick_piece, pieces, facts, found, places=[SMEM, VMEM])
    shared = collect(copies)

    own, other, keep, give = attention_grads(query, out_grad, shared, cont_kv, facts, ring)
    got = swap(give, "kv")
    others = lax.all_gather(other, "core")
    parts = local_call(add_halves, pieces, facts, own, others, places=[SMEM, VMEM, VMEM])
    parts = lax.cond(
        lengths[0] > 0,
        lambda block: lax.all_to_all(block, CHIPS, 0, 0, tiled=True),
        lambda block: block,
        parts,
    )
    send = like((2, *keep.shape[1:]))
    copies, *sends = local_call(sum_pieces, (pieces, *[send] * (ring - 1)), parts, keep, got)
    came = [
        lax.ppermute(block, "kv", [(i, (i + 2 * (n + 1)) % heads) for i in range(heads)])
        for n, block in enumerate(sends)
    ]
    total = collect(copies)
    outs = (
        like((tokens // heads, heads * width)),
        like((tokens // heads, heads * both)),
        like((1, rows, both)),
    )
    return local_call(
        finish, outs, facts, total, keep, got, *came, places=[SMEM] + [VMEM] * (ring + 2)
    )


def solution(mesh):
    fine = jax.sharding.Mesh(mesh.devices.reshape(4, 8, 2, 8), (*GROUP, "kv"))
    placed = (
        P(GROUP, "kv"),
        P(GROUP, "kv"),
        P(GROUP, None, "kv"),
        P(GROUP, "kv"),
        P(GROUP),
        P("kv"),
    )
    return jax.shard_map(
        body,
        mesh=fine,
        in_specs=placed,
        out_specs=(P((*GROUP, "kv"), None), P((*GROUP, "kv"), None), P(GROUP, None, "kv")),
        check_vma=False,
    )
```
